256 devices in a mesh: lon: 16 (over x_hi, z), lat: 8 (over x_lo, y), img: 2 (over core).
Axes of the slice: x: 4 (x_hi: 2, x_lo: 2; x = x_hi * 2 + x_lo), y: 4, z: 8, core: 2. Of those that a mesh axis runs over, the one named last changes fastest.
Arguments:
- control: bfloat16 [2, 128, 256, 320], P('img', 'lat', 'lon'), may hold values from -6 to 6
- conv_weight: bfloat16 [3, 3, 320, 320], replicated, may hold values from -0.109375 to 0.109375
- conv_bias: float32 [320], replicated, may hold values from -3 to 3
- zero_weight: bfloat16 [320, 320], replicated, may hold values from -0.3125 to 0.3125
- strengths: float32 [8], replicated, may hold values from 0.25 to 2
- regions: int32 [2, 8, 16], P('img', None, 'lon'), may hold values from 0 to 7
- control_kv: bfloat16 [320, 2560], replicated, may hold values from -1 to 1
- base_kv: bfloat16 [2, 128, 256, 2560], P('img', 'lat', 'lon'), may hold values from -12 to 12
- queries: bfloat16 [2, 32, 256, 1280], P('img', None, 'lon'), may hold values from -6 to 6
Outputs:
- features: bfloat16 [2, 128, 256, 320], P('img', 'lat', 'lon')
- attended: bfloat16 [2, 32, 256, 1280], P('img', 'lat', 'lon')
The draws below stay inside these ranges and needn't reach their ends.
All inputs are finite; a program needn't handle non-finite values.
Results may differ from the reference program's by a relative error of at most 0.017.
Values may be sent and summed in bfloat16 or wider, within the bound.
A program may use at most 128 MiB of HBM per device.

```python
import math
import jax
import jax.numpy as jnp
from jax import lax

C = 320
HEADS = 20
HDIM = 64
NREG = 8
BAND = 32
IMGS = 2
NLAT = 128
NLON = 256
HD = 1280


def loud_tokens(key):
    key = jax.random.fold_in(key, 41)
    streams = jax.random.split(key, 3)
    number = 12 * IMGS
    picture = jnp.arange(number) % IMGS
    band_row = jax.random.randint(streams[0], (number,), 0, BAND)
    band_column = jax.random.randint(streams[1], (number,), 0, NLON)
    loud_values = jnp.where(jax.random.bernoulli(streams[2], 0.5, (number, HD)), 6.0, -6.0)
    return (picture, band_row, band_column, loud_values)


def draw_queries(key, part):
    own_key = jax.random.fold_in(key, 3)
    extent = (IMGS, BAND, NLON, HD)
    loud_picture, band_row, band_column, loud_values = loud_tokens(own_key)
    entries = jnp.clip(jax.random.normal(own_key, extent), -6.0, 6.0)
    entries = entries.at[loud_picture, band_row, band_column].set(loud_values)
    return entries.astype(jnp.bfloat16)


def draw_base_kv(key, part):
    own_key = jax.random.fold_in(key, 5)
    extent = (IMGS, NLAT, NLON, 2 * HD)
    scaling = jnp.where(jnp.arange(2 * HD) < HD, 1.5, 3.0)
    entries = jnp.clip(jax.random.normal(own_key, extent) * scaling, -12.0, 12.0)
    return entries.astype(jnp.bfloat16)


def draw_control_kv(key, part):
    own_key = jax.random.fold_in(key, 9)
    scaling = jnp.where(jnp.arange(2 * HD) < HD, 0.1, 1.0) * C ** (-0.5)
    entries = jnp.clip(jax.random.normal(own_key, (C, 2 * HD)), -5.0, 5.0) * scaling
    return entries.astype(jnp.bfloat16)


def place_ends(values, stream_key, low, largest):
    longest = values.shape.index(max(values.shape))
    spots = []
    for shift in (0, 1):
        where = [jax.random.randint(jax.random.fold_in(stream_key, axis), (), 0, length) for axis, length in enumerate(values.shape)]
        where[longest] = (where[longest] + shift) % values.shape[longest]
        spots.append(tuple(where))
    return values.at[spots[0]].set(low).at[spots[1]].set(largest)


def shard_levels(rng, dims, shards, smallest, high):
    loudness, own = 1.0, jax.random.fold_in(rng, 6)
    for axis_at, blocks in shards:
        steps = jnp.exp(jax.random.uniform(jax.random.fold_in(own, axis_at), (blocks,), jnp.float32, smallest / len(shards), high / len(shards)))
        loudness = loudness * jnp.repeat(steps, dims[axis_at] // blocks).reshape([-1 if axis == axis_at else 1 for axis in range(len(dims))])
    return loudness


def normal_values(key, dims, width, most, cuts=(), held_as=jnp.bfloat16):
    array = width * jax.random.normal(key, dims, jnp.float32)
    if cuts:
        array = array * shard_levels(key, dims, cuts, -0.22, 0.18)
    return jnp.clip(array, -most, most).astype(held_as)


def setup_inputs(seed: int = 0) -> dict:
    streams_of = jax.random.split(jax.random.key(seed), 10)
    control = normal_values(streams_of[0], (IMGS, NLAT, NLON, C), 1.0, 6.0, ((0, 2), (1, 8), (2, 16)))
    conv_weight = normal_values(streams_of[1], (3, 3, C, C), (9 * C) ** -0.5, 0.109375)
    conv_bias = normal_values(streams_of[2], (C,), 0.5, 3.0, (), jnp.float32)
    zero_weight = normal_values(streams_of[3], (C, C), C ** -0.5, 0.3125)
    strengths = jnp.clip(jnp.exp(jax.random.uniform(streams_of[4], (NREG,), jnp.float32, math.log(0.25), math.log(2.0))), 0.25, 2.0)
    regions = place_ends(jax.random.randint(streams_of[5], (IMGS, NLAT // 16, NLON // 16), 0, NREG), jax.random.fold_in(streams_of[5], 1), 0, NREG - 1).astype(jnp.int32)
    control_kv = draw_control_kv(jax.random.fold_in(streams_of[9], 71), 0)
    base_kv = draw_base_kv(jax.random.fold_in(streams_of[9], 71), 0)
    queries = draw_queries(jax.random.fold_in(streams_of[9], 71), 0)
    return {"control": control, "conv_weight": conv_weight, "conv_bias": conv_bias, "zero_weight": zero_weight, "strengths": strengths, "regions": regions, "control_kv": control_kv, "base_kv": base_kv, "queries": queries}


def control_features(control, conv_weight, conv_bias, zero_weight, strengths, regions):
    padded = jnp.pad(control, ((0, 0), (1, 1), (0, 0), (0, 0)))
    padded = jnp.concatenate([padded[:, :, -1:], padded, padded[:, :, :1]], axis=2)
    height = control.shape[1]
    breadth = control.shape[2]
    convolved = jnp.zeros(control.shape[:3] + (conv_weight.shape[3],), jnp.float32)
    for row_tap in range(3):
        for col_tap in range(3):
            window = padded[:, row_tap:row_tap + height, col_tap:col_tap + breadth].astype(jnp.float32)
            convolved = convolved + jnp.einsum('bhwc,cd->bhwd', window, conv_weight[row_tap, col_tap].astype(jnp.float32))
    active = jax.nn.silu(convolved + conv_bias[None, None, None, :]).astype(jnp.bfloat16)
    branch = jnp.einsum('bhwc,cd->bhwd', active.astype(jnp.float32), zero_weight.astype(jnp.float32))
    cell_region = jnp.repeat(jnp.repeat(regions, 16, axis=1), 16, axis=2)
    cell_strength = strengths[cell_region]
    return (control.astype(jnp.float32) + cell_strength[..., None] * branch).astype(jnp.bfloat16)


def one_head(operands):
    query_head, key_head, value_head = operands
    scores = jnp.dot(query_head, key_head.T, preferred_element_type=jnp.float32) * HDIM ** -0.5
    exp_scores = jnp.exp(scores - jnp.max(scores, axis=1, keepdims=True))
    denominator = jnp.sum(exp_scores, axis=1, keepdims=True)
    numerator = jnp.dot(exp_scores.astype(jnp.bfloat16), value_head, preferred_element_type=jnp.float32)
    return (numerator / denominator).astype(jnp.bfloat16)


def reference(control, conv_weight, conv_bias, zero_weight, strengths, regions, control_kv, base_kv, queries):
    features = control_features(control, conv_weight, conv_bias, zero_weight, strengths, regions)
    kv_delta = jnp.einsum('bhwc,cd->bhwd', features.astype(jnp.float32), control_kv.astype(jnp.float32))
    key_value = (base_kv.astype(jnp.float32) + kv_delta).astype(jnp.bfloat16)
    keys = key_value[..., :HD]
    values = key_value[..., HD:]
    token_keys = keys.reshape(IMGS, NLAT * NLON, HEADS, HDIM).transpose(0, 2, 1, 3).reshape(IMGS * HEADS, NLAT * NLON, HDIM)
    token_values = values.reshape(IMGS, NLAT * NLON, HEADS, HDIM).transpose(0, 2, 1, 3).reshape(IMGS * HEADS, NLAT * NLON, HDIM)
    token_queries = queries.reshape(IMGS, BAND * NLON, HEADS, HDIM).transpose(0, 2, 1, 3).reshape(IMGS * HEADS, BAND * NLON, HDIM)
    outputs = lax.map(one_head, (token_queries, token_keys, token_values))
    attended = outputs.reshape(IMGS, HEADS, BAND * NLON, HDIM).transpose(0, 2, 1, 3).reshape(IMGS, BAND, NLON, HD)
    return features, attended
```

```python
import jax
import jax.numpy as jnp
from jax import lax
from jax.experimental import pallas as pl
from jax.experimental.pallas import tpu as pltpu
from jax.sharding import PartitionSpec as P

F32, BF16 = jnp.float32, jnp.bfloat16
MESH = pl.DeviceIdType.MESH
NX, NY, NZ = 4, 4, 8
LON, LAT = 16, 8
TOK = 256
C = 320
HD = 64
HEADS = 20
PER = HEADS // NY
WIDE = HEADS * HD
PAIRS = NX * NY // 2
PAY_ROWS = TOK
O_ROWS = HD + 16
FIRST_TILES = (0, 2, 5, 7)
OTHER_TILES = (1, 3, 4, 6, 8, 9)


def dot(a, b):
    return jnp.dot(a, b, preferred_element_type=F32)


def kernel(
    ctl, cw, bias, zw, strg, reg, wkv, base, qin,
    feat, att,
    hs, hr, xs, pay, kv, qt, qb, s0, s1, osend, orecv, ct, fo, fr,
    h_s, h_r, q_s, q_r, y_s, y_r, x_s, x_r, w_s, w_r, o_s, o_r, f_s, f_r,
):
    lon, lat = lax.axis_index("lon"), lax.axis_index("lat")
    xh, z = lon // NZ, lon % NZ
    xl, y = lat // NY, lat % NY
    x = xh * 2 + xl
    right, left = (x + 1) % NX, (x + 3) % NX

    def at(px, py, pz):
        return {"lon": (px // 2) * NZ + pz, "lat": (px % 2) * NY + py}

    def remote(src, dst, send, recv, where):
        return pltpu.make_async_remote_copy(
            src_ref=src, dst_ref=dst, send_sem=send, recv_sem=recv, device_id=where, device_id_type=MESH
        )

    west, east = (lon + LON - 1) % LON, (lon + 1) % LON
    north, south = (lat + LAT - 1) % LAT, (lat + 1) % LAT
    around = (
        (west, north), (west, lat), (west, south),
        (east, north), (east, lat), (east, south),
        (lon, north), (lon, south),
    )

    def halo(k):
        src = hs.at[0] if k < 3 else hs.at[1] if k < 6 else ctl.at[pl.ds(0 if k == 6 else TOK - 16, 16)]
        return remote(src, hr.at[k], h_s.at[k], h_r.at[k], {"lon": around[k][0], "lat": around[k][1]})

    def q_send(j, k):
        return remote(qt.at[y * PER + j], qb.at[j, z], q_s.at[j, k], q_r.at[j, k], at(x, y, (z + k) % NZ))

    def q_recv(j, k):
        src = (z + NZ - k) % NZ
        return remote(qb.at[j, src], qb.at[j, src], q_s.at[j, k], q_r.at[j, k], at(x, y, src))

    def y_send(j, k):
        to = (y + k) % NY
        return remote(pay.at[j, to], kv.at[j, x, y], y_s.at[j, k], y_r.at[j, k], at(x, to, z))

    def y_recv(j, k):
        src = (y + NY - k) % NY
        return remote(kv.at[j, x, src], kv.at[j, x, src], y_s.at[j, k], y_r.at[j, k], at(x, src, z))

    def x_send(j, k):
        to = right if k == 0 else left
        return remote(kv.at[j, x], kv.at[j, x], x_s.at[j, k], x_r.at[j, k], at(to, y, z))

    def x_recv(j, k):
        src = left if k == 0 else right
        return remote(kv.at[j, src], kv.at[j, src], x_s.at[j, k], x_r.at[j, k], at(src, y, z))

    def w_send(j, k):
        slab, to = (left, right) if k == 0 else (right, left)
        ref = kv.at[j, slab, pl.ds(2 * k, 2)]
        return remote(ref, ref, w_s.at[j, k], w_r.at[j, k], at(to, y, z))

    def w_recv(j, k):
        ref = kv.at[j, (x + 2) % NX, pl.ds(2 * k, 2)]
        return remote(ref, ref, w_s.at[j, k], w_r.at[j, k], at(left if k == 0 else right, y, z))

    def o_send(j, k):
        return remote(osend.at[j, k], orecv.at[j, k], o_s.at[j, k], o_r.at[j, k], at(x, y, (z + k) % NZ))

    def f_send(k):
        to = (y + k) % NY
        return remote(fo.at[to], fr.at[y], f_s.at[k], f_r.at[k], at(x, to, z))

    def f_recv(k):
        src = (y + NY - k) % NY
        return remote(fr.at[src], fr.at[src], f_s.at[k], f_r.at[k], at(x, src, z))

    barrier = pltpu.get_barrier_semaphore()
    partners = [at(right, y, z), at(left, y, z)]
    partners += [at(x, (y + k) % NY, z) for k in range(1, NY)]
    partners += [at(x, y, (z + k) % NZ) for k in range(1, NZ)]
    partners += [{"lon": a, "lat": b} for a, b in around]
    for who in partners:
        pl.semaphore_signal(barrier, inc=1, device_id=who, device_id_type=MESH)

    row16 = lax.broadcasted_iota(jnp.int32, (16, TOK), 0)
    col16 = lax.broadcasted_iota(jnp.int32, (16, TOK), 1)
    for side, off in ((0, 0), (1, 15)):
        pick = jnp.where(col16 == row16 * 16 + off, 1.0, 0.0).astype(BF16)
        hs[side] = dot(pick, ctl[...]).astype(BF16)
    pl.semaphore_wait(barrier, len(partners))
    for k in range(8):
        halo(k).start()

    for p in range(HEADS // 2):
        tile = qin[pl.ds(pl.multiple_of(xl * TOK, TOK), TOK), p * 128 : (p + 1) * 128].astype(F32)
        turned = (tile.T * (HD**-0.5)).astype(BF16)
        qt[2 * p] = turned[:HD]
        qt[2 * p + 1] = turned[HD:]

    def q_out(j, _):
        for k in (4, 3, 5, 2, 6, 1, 7):
            q_send(j, k).start()
        qb[j, z] = qt[y * PER + j]
        return 0

    lax.fori_loop(0, PER, q_out, 0)

    for k in range(8):
        halo(k).wait_recv()
    top = hr[7].astype(F32) * jnp.where(lat > 0, 1.0, 0.0)
    bottom = hr[6].astype(F32) * jnp.where(lat < LAT - 1, 1.0, 0.0)
    middle = jnp.concatenate([top, ctl[...].astype(F32), bottom], axis=0)
    tall = TOK + 32
    row = lax.broadcasted_iota(jnp.int32, (tall, 48), 0)
    pos = lax.broadcasted_iota(jnp.int32, (tall, 48), 1)
    first = jnp.where(lat > 0, 15, 16)
    last = jnp.where(lat < LAT - 1, 32, 31)
    wanted = (pos == row // 16 + 15) & (pos >= first) & (pos <= last)
    rows = lax.broadcasted_iota(jnp.int32, (tall, C), 0) % 16
    for tap, slots, edge, turn in ((0, (5, 4, 3), 0, 1), (2, (2, 1, 0), 15, tall - 1)):
        columns = jnp.concatenate([hr[s] for s in slots], axis=0)
        spread = dot(jnp.where(wanted & (row % 16 == edge), 1.0, 0.0).astype(BF16), columns)
        xs[tap] = jnp.where(rows == edge, spread, pltpu.roll(middle, turn, 0)).astype(BF16)
    xs[1] = middle.astype(BF16)
    total = jnp.zeros((TOK, C), F32)
    for dr in range(3):
        for dc in range(3):
            total += dot(xs[dc, 16 * dr : 16 * dr + TOK], cw[3 * dr + dc])
    total += bias[...]
    active = (total / (1.0 + jnp.exp(-total))).astype(BF16)
    branch = dot(active, zw[...])
    strength = strg[reg[lat]]
    features = (ctl[...].astype(F32) + strength * branch).astype(BF16)
    feat[...] = features

    low = lax.broadcasted_iota(jnp.int32, (128, 128), 1) < HD

    def project(p):
        def part(col):
            out = base[:, col : col + 128].astype(F32) + dot(feat[...], wkv[:, col : col + 128])
            return out.astype(BF16).astype(F32)

        keys, turned = part(p * 128), part(WIDE + p * 128).T
        a, b = keys[:128], keys[128:]
        packed = (jnp.where(low, a, pltpu.roll(b, HD, 1)), jnp.where(low, pltpu.roll(a, HD, 1), b))
        for half in range(2):
            g, j = divmod(2 * p + half, PER)
            pay[j, g, 0:128] = packed[half].astype(BF16)
            pay[j, g, 128:192] = turned[half * HD : (half + 1) * HD, :128].astype(BF16)
            pay[j, g, 192:256] = turned[half * HD : (half + 1) * HD, 128:].astype(BF16)

    def y_out(j):
        for k in (2, 1, 3):
            y_send(j, k).start()
        kv[j, x, y] = pay[j, y]

    for p in FIRST_TILES:
        project(p)
    y_out(0)
    for p in OTHER_TILES:
        project(p)
    lax.fori_loop(1, PER, lambda j, _: (y_out(j), 0)[1], 0)

    def spread_start(j):
        for k in range(1, NY):
            y_recv(j, k).wait_recv()
        for k in range(2):
            x_send(j, k).start()

    def spread_more(j):
        for k in range(2):
            x_recv(j, k).wait_recv()
        for k in range(2):
            w_send(j, k).start()

    def spread_end(j):
        for k in range(2):
            w_recv(j, k).wait_recv()
        for k in range(1, NZ):
            q_recv(j, k).wait_recv()

    nothing = jnp.zeros((HD, TOK), BF16)
    ones = jnp.ones((16, TOK), BF16)

    def weights_of(j, k):
        q = qb[j, (z + k) % NZ]
        return jnp.concatenate(
            [jnp.concatenate([q, nothing], axis=0), jnp.concatenate([nothing, q], axis=0)], axis=1
        )

    def score(j, w, p, scores, peak):
        keys = kv[j, p // 2, 2 * (p % 2) : 2 * (p % 2) + 2, 0:128].reshape(TOK, 128)
        s = dot(keys, w)
        for half in range(2):
            part = s[:, half * TOK : (half + 1) * TOK]
            scores[(2 * p + half) * TOK : (2 * p + half + 1) * TOK] = part
            peak = jnp.maximum(peak, part.reshape(TOK // 8, 8, TOK).max(0))
        return peak

    def gather(j, p, scores, peak, acc):
        for half in range(2):
            s = scores[(2 * p + half) * TOK : (2 * p + half + 1) * TOK]
            weights = jnp.exp(s - peak).astype(BF16)
            begin = 128 + half * HD
            v = jnp.concatenate(
                [kv[j, p // 2, 2 * (p % 2) + u, begin : begin + HD] for u in range(2)], axis=1
            )
            acc += dot(jnp.concatenate([v, ones], axis=0), weights)
        return acc

    low_peak = jnp.full((8, TOK), -jnp.inf, F32)

    def packed_result(acc, peak):
        sums = acc[HD : HD + 1]
        log_sum = peak + jnp.log(sums)
        hi = log_sum.astype(BF16).astype(F32)
        mid = (log_sum - hi).astype(BF16).astype(F32)
        lo = log_sum - hi - mid
        r = lax.broadcasted_iota(jnp.int32, (16, TOK), 0)
        stats = jnp.where(r == 0, hi, jnp.where(r == 1, mid, jnp.where(r == 2, lo, 0.0)))
        return jnp.concatenate([acc[:HD] * (1.0 / sums), stats], axis=0).astype(BF16)

    def both(j, nj, nk, ready, coming, peak):
        w = weights_of(nj, nk)
        next_peak, acc = low_peak, jnp.zeros((O_ROWS, TOK), F32)
        for p in range(PAIRS):
            next_peak = score(nj, w, p, coming, next_peak)
            acc = gather(j, p, ready, peak, acc)
        return packed_result(acc, peak), next_peak.max(0, keepdims=True)

    def join(j):
        parts, logs = [], []
        for k in range(NZ):
            if k > 0:
                o_send(j, k).wait_recv()
            logs.append(orecv[j, k, HD : HD + 16].astype(F32)[0:3].sum(0, keepdims=True))
        top_log = logs[0]
        for other in logs[1:]:
            top_log = jnp.maximum(top_log, other)
        out, whole = jnp.zeros((HD, TOK), F32), jnp.zeros((1, TOK), F32)
        for k in range(NZ):
            share = jnp.exp(logs[k] - top_log)
            whole += share
            out += orecv[j, k, 0:HD].astype(F32) * share
        ct[j] = out * (1.0 / whole)

    spread_start(0)
    spread_more(0)
    spread_end(0)
    w = weights_of(0, 4)
    peak = low_peak
    for p in range(PAIRS):
        peak = score(0, w, p, s0, peak)
    peak = peak.max(0, keepdims=True)

    def step(n, peak):
        j, i = n // 4, n % 4
        more = j < PER - 1

        @pl.when((i == 0) & more)
        def _():
            spread_start(j + 1)

        @pl.when((i == 2) & more)
        def _():
            spread_more(j + 1)

        @pl.when((i == 1) & (j > 0))
        def _():
            join(j - 1)

        result, peak = both(j, j, 3 - i, s0, s1, peak)
        osend[j, 4 + i] = result
        o_send(j, 4 + i).start()

        @pl.when((i == 3) & more)
        def _():
            spread_end(j + 1)

        nj = jnp.where((i == 3) & more, j + 1, j)
        nk = jnp.where(i == 3, 4, 5 + i)
        result, peak = both(j, nj, nk, s1, s0, peak)

        @pl.when(i < 3)
        def _():
            osend[j, 3 - i] = result
            o_send(j, 3 - i).start()

        @pl.when(i == 3)
        def _():
            orecv[j, 0] = result

        return peak

    lax.fori_loop(0, 4 * PER, step, peak)
    join(PER - 1)

    for t in range(3):
        if t < 2:
            turned = jnp.concatenate([ct[2 * t], ct[2 * t + 1]], axis=0).T
        else:
            turned = jnp.concatenate([ct[4], jnp.zeros((HD, TOK), F32)], axis=0).T
        for g in range(NY):
            fo[g, :, t * 128 : (t + 1) * 128] = turned[g * 64 : (g + 1) * 64].astype(BF16)
    for k in (2, 1, 3):
        f_send(k).start()
    fr[y] = fo[y]
    for k in range(1, NY):
        f_recv(k).wait_recv()
    att[...] = jnp.concatenate([fr[g][:, :C].astype(F32) for g in range(NY)], axis=1).astype(BF16)

    for k in range(8):
        halo(k).wait_send()

    def drain(j, _):
        for k in range(1, NZ):
            q_send(j, k).wait_send()
            o_send(j, k).wait_send()
        for k in range(1, NY):
            y_send(j, k).wait_send()
        for k in range(2):
            x_send(j, k).wait_send()
            w_send(j, k).wait_send()
        return 0

    lax.fori_loop(0, PER, drain, 0)
    for k in range(1, NY):
        f_send(k).wait_send()


def body(control, conv_weight, conv_bias, zero_weight, strengths, regions, control_kv, base_kv, queries):
    vmem = pl.BlockSpec(memory_space=pltpu.VMEM)
    smem = pl.BlockSpec(memory_space=pltpu.SMEM)
    dma = pltpu.SemaphoreType.DMA
    features, attended = pl.pallas_call(
        kernel,
        out_shape=[
            jax.ShapeDtypeStruct((TOK, C), BF16),
            jax.ShapeDtypeStruct((64, WIDE), BF16),
        ],
        in_specs=[vmem, vmem, vmem, vmem, smem, smem, vmem, vmem, vmem],
        out_specs=[vmem, vmem],
        scratch_shapes=[
            pltpu.VMEM((2, 16, C), BF16),
            pltpu.VMEM((8, 16, C), BF16),
            pltpu.VMEM((3, TOK + 32, C), BF16),
            pltpu.VMEM((PER, NY, PAY_ROWS, 128), BF16),
            pltpu.VMEM((PER, NX, NY, PAY_ROWS, 128), BF16),
            pltpu.VMEM((HEADS, HD, TOK), BF16),
            pltpu.VMEM((PER, NZ, HD, TOK), BF16),
            pltpu.VMEM((NX * NY * TOK, TOK), F32),
            pltpu.VMEM((NX * NY * TOK, TOK), F32),
            pltpu.VMEM((PER, NZ, O_ROWS, TOK), BF16),
            pltpu.VMEM((PER, NZ, O_ROWS, TOK), BF16),
            pltpu.VMEM((PER, HD, TOK), F32),
            pltpu.VMEM((NY, 64, 384), BF16),
            pltpu.VMEM((NY, 64, 384), BF16),
            dma((8,)), dma((8,)),
            dma((PER, NZ)), dma((PER, NZ)),
            dma((PER, NY)), dma((PER, NY)),
            dma((PER, 2)), dma((PER, 2)),
            dma((PER, 2)), dma((PER, 2)),
            dma((PER, NZ)), dma((PER, NZ)),
            dma((NY,)), dma((NY,)),
        ],
        compiler_params=pltpu.CompilerParams(
            collective_id=0, has_side_effects=True, vmem_limit_bytes=48 * 2**20
        ),
    )(
        control.reshape(TOK, C),
        conv_weight.reshape(9, C, C),
        conv_bias.reshape(1, C),
        zero_weight,
        strengths,
        regions.reshape(-1),
        control_kv,
        base_kv.reshape(TOK, 2 * WIDE),
        queries.reshape(2 * TOK, WIDE),
    )
    return features.reshape(1, 16, 16, C), attended.reshape(1, 4, 16, WIDE)


def solution(mesh):
    in_specs = (
        P("img", "lat", "lon", None),
        P(),
        P(),
        P(),
        P(),
        P("img", None, "lon"),
        P(),
        P("img", "lat", "lon", None),
        P("img", None, "lon", None),
    )
    out_specs = (P("img", "lat", "lon", None), P("img", "lat", "lon", None))
    return jax.shard_map(body, mesh=mesh, in_specs=in_specs, out_specs=out_specs, check_vma=False)
```

```python
import jax
import jax.numpy as jnp
from jax import lax
from jax.experimental import pallas as pl
from jax.experimental.pallas import tpu as pltpu
from jax.sharding import PartitionSpec as P

F32, BF16 = jnp.float32, jnp.bfloat16
MESH = pl.DeviceIdType.MESH
NX, NY, NZ = 4, 4, 8
LON, LAT = 16, 8
TOK = 256
C = 320
HD = 64
HEADS = 20
PER = HEADS // NY
WIDE = HEADS * HD
PAIRS = NX * NY // 2
PAY_ROWS = TOK
O_ROWS = HD + 16
FIRST_TILES = (0, 2, 5, 7)
OTHER_TILES = (1, 3, 4, 6, 8, 9)


def dot(a, b):
    return jnp.dot(a, b, preferred_element_type=F32)


def kernel(
    ctl_h, cw_h, bias_h, zw_h, strg_h, reg_h, wkv_h, base_h, qin_h,
    feat, att,
    ctl, cw, bias, zw, strg, reg, wkv, base, qin,
    hs, hr, xs, pay, kv, qt, qb, s0, s1, osend, orecv, ct, fo, fr,
    in_s, h_s, h_r, q_s, q_r, y_s, y_r, x_s, x_r, w_s, w_r, o_s, o_r, f_s, f_r,
):
    lon, lat = lax.axis_index("lon"), lax.axis_index("lat")
    xh, z = lon // NZ, lon % NZ
    xl, y = lat // NY, lat % NY
    x = xh * 2 + xl
    right, left = (x + 1) % NX, (x + 3) % NX

    def at(px, py, pz):
        return {"lon": (px // 2) * NZ + pz, "lat": (px % 2) * NY + py}

    def remote(src, dst, send, recv, where):
        return pltpu.make_async_remote_copy(
            src_ref=src, dst_ref=dst, send_sem=send, recv_sem=recv, device_id=where, device_id_type=MESH
        )

    west, east = (lon + LON - 1) % LON, (lon + 1) % LON
    north, south = (lat + LAT - 1) % LAT, (lat + 1) % LAT
    around = (
        (west, north), (west, lat), (west, south),
        (east, north), (east, lat), (east, south),
        (lon, north), (lon, south),
    )

    def halo(k):
        src = hs.at[0] if k < 3 else hs.at[1] if k < 6 else ctl.at[pl.ds(0 if k == 6 else TOK - 16, 16)]
        return remote(src, hr.at[k], h_s.at[k], h_r.at[k], {"lon": around[k][0], "lat": around[k][1]})

    def q_part(step, k):
        tile = (z + NZ - step) % NZ if k == 0 else (z + step) % NZ
        if step < 3:
            return qb.at[tile]
        return qb.at[tile, pl.ds(0, 2)] if k == 0 else qb.at[tile, pl.ds(2, 3)]

    def q_send(step, k):
        ref = q_part(step, k)
        to = (z + 1) % NZ if k == 0 else (z + NZ - 1) % NZ
        return remote(ref, ref, q_s.at[step, k], q_r.at[step, k], at(x, y, to))

    def q_recv(step, k):
        tile = (z + NZ - step - 1) % NZ if k == 0 else (z + step + 1) % NZ
        ref = qb.at[tile] if step < 3 else qb.at[tile, pl.ds(0, 2)] if k == 0 else qb.at[tile, pl.ds(2, 3)]
        src = (z + NZ - 1) % NZ if k == 0 else (z + 1) % NZ
        return remote(ref, ref, q_s.at[step, k], q_r.at[step, k], at(x, y, src))

    def q_step(step):
        for k in range(2):
            if step > 0:
                q_recv(step - 1, k).wait_recv()
            q_send(step, k).start()

    def y_send(j, k):
        to = (y + k) % NY
        return remote(pay.at[j, to], kv.at[j, x, y], y_s.at[j, k], y_r.at[j, k], at(x, to, z))

    def y_recv(j, k):
        src = (y + NY - k) % NY
        return remote(kv.at[j, x, src], kv.at[j, x, src], y_s.at[j, k], y_r.at[j, k], at(x, src, z))

    def x_send(j, k, part):
        to = right if k == 0 else left
        ref = kv.at[j, x, pl.ds(2 * (k ^ part), 2)]
        return remote(ref, ref, x_s.at[j, k, part], x_r.at[j, k, part], at(to, y, z))

    def x_recv(j, k, part):
        src = left if k == 0 else right
        ref = kv.at[j, src, pl.ds(2 * (k ^ part), 2)]
        return remote(ref, ref, x_s.at[j, k, part], x_r.at[j, k, part], at(src, y, z))

    def w_send(j, k):
        slab, to = (left, right) if k == 0 else (right, left)
        ref = kv.at[j, slab, pl.ds(2 * k, 2)]
        return remote(ref, ref, w_s.at[j, k], w_r.at[j, k], at(to, y, z))

    def w_recv(j, k):
        ref = kv.at[j, (x + 2) % NX, pl.ds(2 * k, 2)]
        return remote(ref, ref, w_s.at[j, k], w_r.at[j, k], at(left if k == 0 else right, y, z))

    def o_send(j, k):
        return remote(osend.at[j, k], orecv.at[j, k], o_s.at[j, k], o_r.at[j, k], at(x, y, (z + k) % NZ))

    def f_send(k):
        to = (y + k) % NY
        return remote(fo.at[to], fr.at[y], f_s.at[k], f_r.at[k], at(x, to, z))

    def f_recv(k):
        src = (y + NY - k) % NY
        return remote(fr.at[src], fr.at[src], f_s.at[k], f_r.at[k], at(x, src, z))

    first_tile = (y * PER) // 2
    rows_q = pl.ds(pl.multiple_of(xl * TOK, TOK), TOK)
    lanes_q = pl.ds(pl.multiple_of(first_tile * 128, 128), 384)
    pairs_in = (
        (ctl_h, ctl), (qin_h.at[rows_q, lanes_q], qin), (cw_h, cw), (bias_h, bias), (zw_h, zw),
        (strg_h, strg), (reg_h, reg), (base_h, base), (wkv_h, wkv),
    )
    fetch = [pltpu.make_async_copy(a, b, in_s.at[n]) for n, (a, b) in enumerate(pairs_in)]
    for copy in fetch:
        copy.start()

    barrier = pltpu.get_barrier_semaphore()
    partners = [at(right, y, z), at(left, y, z)]
    partners += [at(x, (y + k) % NY, z) for k in range(1, NY)]
    partners += [at(x, y, (z + k) % NZ) for k in range(1, NZ)]
    partners += [{"lon": a, "lat": b} for a, b in around]
    for who in partners:
        pl.semaphore_signal(barrier, inc=1, device_id=who, device_id_type=MESH)

    fetch[0].wait()
    row16 = lax.broadcasted_iota(jnp.int32, (16, TOK), 0)
    col16 = lax.broadcasted_iota(jnp.int32, (16, TOK), 1)
    for side, off in ((0, 0), (1, 15)):
        pick = jnp.where(col16 == row16 * 16 + off, 1.0, 0.0).astype(BF16)
        hs[side] = dot(pick, ctl[...]).astype(BF16)

    fetch[1].wait()
    for t in range(3):
        turned = (qin[:, t * 128 : (t + 1) * 128].astype(F32).T * (HD**-0.5)).astype(BF16)
        qt[2 * t] = turned[:HD]
        qt[2 * t + 1] = turned[HD:]
    for j in range(PER):
        qb[z, j] = qt[(y * PER) % 2 + j]

    pl.semaphore_wait(barrier, len(partners))
    for k in range(8):
        halo(k).start()
    q_step(0)

    for k in range(8):
        halo(k).wait_recv()
    top = hr[7].astype(F32) * jnp.where(lat > 0, 1.0, 0.0)
    bottom = hr[6].astype(F32) * jnp.where(lat < LAT - 1, 1.0, 0.0)
    middle = jnp.concatenate([top, ctl[...].astype(F32), bottom], axis=0)
    tall = TOK + 32
    row = lax.broadcasted_iota(jnp.int32, (tall, 48), 0)
    pos = lax.broadcasted_iota(jnp.int32, (tall, 48), 1)
    first = jnp.where(lat > 0, 15, 16)
    last = jnp.where(lat < LAT - 1, 32, 31)
    wanted = (pos == row // 16 + 15) & (pos >= first) & (pos <= last)
    rows = lax.broadcasted_iota(jnp.int32, (tall, C), 0) % 16
    for tap, slots, edge, turn in ((0, (5, 4, 3), 0, 1), (2, (2, 1, 0), 15, tall - 1)):
        columns = jnp.concatenate([hr[s] for s in slots], axis=0)
        spread = dot(jnp.where(wanted & (row % 16 == edge), 1.0, 0.0).astype(BF16), columns)
        xs[tap] = jnp.where(rows == edge, spread, pltpu.roll(middle, turn, 0)).astype(BF16)
    xs[1] = middle.astype(BF16)
    for n in (2, 3, 4, 5, 6):
        fetch[n].wait()
    total = jnp.zeros((TOK, C), F32)
    for dr in range(3):
        for dc in range(3):
            total += dot(xs[dc, 16 * dr : 16 * dr + TOK], cw[3 * dr + dc])
    total += bias[...].reshape(1, C)
    active = (total / (1.0 + jnp.exp(-total))).astype(BF16)
    branch = dot(active, zw[...])
    strength = strg[reg[lat]]
    features = (ctl[...].astype(F32) + strength * branch).astype(BF16)
    feat[...] = features
    q_step(1)

    low = lax.broadcasted_iota(jnp.int32, (128, 128), 1) < HD

    def project(p):
        def part(col):
            out = base[:, col : col + 128].astype(F32) + dot(feat[...], wkv[:, col : col + 128])
            return out.astype(BF16).astype(F32)

        keys, turned = part(p * 128), part(WIDE + p * 128).T
        a, b = keys[:128], keys[128:]
        packed = (jnp.where(low, a, pltpu.roll(b, HD, 1)), jnp.where(low, pltpu.roll(a, HD, 1), b))
        for half in range(2):
            g, j = divmod(2 * p + half, PER)
            pay[j, g, 0:128] = packed[half].astype(BF16)
            pay[j, g, 128:192] = turned[half * HD : (half + 1) * HD, :128].astype(BF16)
            pay[j, g, 192:256] = turned[half * HD : (half + 1) * HD, 128:].astype(BF16)

    def y_out(j):
        for k in (2, 1, 3):
            y_send(j, k).start()
        kv[j, x, y] = pay[j, y]

    fetch[7].wait()
    fetch[8].wait()
    for p in FIRST_TILES:
        project(p)
    y_out(0)
    for p in OTHER_TILES:
        project(p)
    q_step(2)

    def spread_start(j):
        for k in range(1, NY):
            y_recv(j, k).wait_recv()
        for part in range(2):
            for k in range(2):
                x_send(j, k, part).start()

    def spread_more(j):
        for k in range(2):
            x_recv(j, k, 0).wait_recv()
            w_send(j, k).start()

    def spread_end(j):
        for k in range(2):
            x_recv(j, k, 1).wait_recv()
            w_recv(j, k).wait_recv()

    nothing = jnp.zeros((HD, TOK), BF16)
    ones = jnp.ones((16, TOK), BF16)

    def weights_of(j, k):
        q = qb[(z + k) % NZ, j]
        return jnp.concatenate(
            [jnp.concatenate([q, nothing], axis=0), jnp.concatenate([nothing, q], axis=0)], axis=1
        )

    def score(j, w, p, scores, peak):
        keys = kv[j, p // 2, 2 * (p % 2) : 2 * (p % 2) + 2, 0:128].reshape(TOK, 128)
        s = dot(keys, w)
        for half in range(2):
            part = s[:, half * TOK : (half + 1) * TOK]
            scores[(2 * p + half) * TOK : (2 * p + half + 1) * TOK] = part
            peak = jnp.maximum(peak, part.reshape(TOK // 8, 8, TOK).max(0))
        return peak

    def gather(j, p, scores, peak, acc):
        for half in range(2):
            s = scores[(2 * p + half) * TOK : (2 * p + half + 1) * TOK]
            weights = jnp.exp(s - peak).astype(BF16)
            begin = 128 + half * HD
            v = jnp.concatenate(
                [kv[j, p // 2, 2 * (p % 2) + u, begin : begin + HD] for u in range(2)], axis=1
            )
            acc += dot(jnp.concatenate([v, ones], axis=0), weights)
        return acc

    low_peak = jnp.full((8, TOK), -jnp.inf, F32)

    def packed_result(acc, peak):
        sums = acc[HD : HD + 1]
        log_sum = peak + jnp.log(sums)
        hi = log_sum.astype(BF16).astype(F32)
        mid = (log_sum - hi).astype(BF16).astype(F32)
        lo = log_sum - hi - mid
        r = lax.broadcasted_iota(jnp.int32, (16, TOK), 0)
        stats = jnp.where(r == 0, hi, jnp.where(r == 1, mid, jnp.where(r == 2, lo, 0.0)))
        return jnp.concatenate([acc[:HD] * (1.0 / sums), stats], axis=0).astype(BF16)

    def both(j, nj, nk, ready, coming, peak):
        w = weights_of(nj, nk)
        next_peak, acc = low_peak, jnp.zeros((O_ROWS, TOK), F32)
        for p in range(PAIRS):
            next_peak = score(nj, w, p, coming, next_peak)
            acc = gather(j, p, ready, peak, acc)
        return packed_result(acc, peak), next_peak.max(0, keepdims=True)

    def join(j):
        parts, logs = [], []
        for k in range(NZ):
            if k > 0:
                o_send(j, k).wait_recv()
            logs.append(orecv[j, k, HD : HD + 16].astype(F32)[0:3].sum(0, keepdims=True))
        top_log = logs[0]
        for other in logs[1:]:
            top_log = jnp.maximum(top_log, other)
        out, whole = jnp.zeros((HD, TOK), F32), jnp.zeros((1, TOK), F32)
        for k in range(NZ):
            share = jnp.exp(logs[k] - top_log)
            whole += share
            out += orecv[j, k, 0:HD].astype(F32) * share
        ct[j] = out * (1.0 / whole)

    spread_start(0)
    lax.fori_loop(1, PER, lambda j, _: (y_out(j), 0)[1], 0)
    spread_more(0)
    spread_start(1)
    q_step(3)
    spread_end(0)
    for k in range(2):
        q_recv(3, k).wait_recv()
    w = weights_of(0, 4)
    peak = low_peak
    for p in range(PAIRS):
        peak = score(0, w, p, s0, peak)
    peak = peak.max(0, keepdims=True)

    def step(n, peak):
        j, i = n // 4, n % 4
        more = j < PER - 1

        @pl.when((i == 1) & more)
        def _():
            spread_more(j + 1)

        @pl.when((i == 1) & (j < PER - 2))
        def _():
            spread_start(j + 2)

        @pl.when((i == 2) & (j > 0))
        def _():
            join(j - 1)

        result, peak = both(j, j, 3 - i, s0, s1, peak)
        osend[j, 4 + i] = result
        o_send(j, 4 + i).start()

        @pl.when((i == 3) & more)
        def _():
            spread_end(j + 1)

        nj = jnp.where((i == 3) & more, j + 1, j)
        nk = jnp.where(i == 3, 4, 5 + i)
        result, peak = both(j, nj, nk, s1, s0, peak)

        @pl.when(i < 3)
        def _():
            osend[j, 3 - i] = result
            o_send(j, 3 - i).start()

        @pl.when(i == 3)
        def _():
            orecv[j, 0] = result

        return peak

    lax.fori_loop(0, 4 * PER, step, peak)
    join(PER - 1)

    for t in range(3):
        if t < 2:
            turned = jnp.concatenate([ct[2 * t], ct[2 * t + 1]], axis=0).T
        else:
            turned = jnp.concatenate([ct[4], jnp.zeros((HD, TOK), F32)], axis=0).T
        for g in range(NY):
            fo[g, :, t * 128 : (t + 1) * 128] = turned[g * 64 : (g + 1) * 64].astype(BF16)
    for k in (2, 1, 3):
        f_send(k).start()
    fr[y] = fo[y]
    for k in range(1, NY):
        f_recv(k).wait_recv()
    att[...] = jnp.concatenate([fr[g][:, :C].astype(F32) for g in range(NY)], axis=1).astype(BF16)

    for k in range(8):
        halo(k).wait_send()

    for step in range(4):
        for k in range(2):
            q_send(step, k).wait_send()

    def drain(j, _):
        for k in range(1, NZ):
            o_send(j, k).wait_send()
        for k in range(1, NY):
            y_send(j, k).wait_send()
        for k in range(2):
            x_send(j, k, 0).wait_send()
            x_send(j, k, 1).wait_send()
            w_send(j, k).wait_send()
        return 0

    lax.fori_loop(0, PER, drain, 0)
    for k in range(1, NY):
        f_send(k).wait_send()


def body(control, conv_weight, conv_bias, zero_weight, strengths, regions, control_kv, base_kv, queries):
    vmem = pl.BlockSpec(memory_space=pltpu.VMEM)
    hbm = pl.BlockSpec(memory_space=pltpu.HBM)
    dma = pltpu.SemaphoreType.DMA
    features, attended = pl.pallas_call(
        kernel,
        out_shape=[
            jax.ShapeDtypeStruct((TOK, C), BF16),
            jax.ShapeDtypeStruct((64, WIDE), BF16),
        ],
        in_specs=[hbm] * 9,
        out_specs=[vmem, vmem],
        scratch_shapes=[
            pltpu.VMEM((TOK, C), BF16),
            pltpu.VMEM((9, C, C), BF16),
            pltpu.VMEM((C,), F32),
            pltpu.VMEM((C, C), BF16),
            pltpu.SMEM((8,), F32),
            pltpu.SMEM((8,), jnp.int32),
            pltpu.VMEM((C, 2 * WIDE), BF16),
            pltpu.VMEM((TOK, 2 * WIDE), BF16),
            pltpu.VMEM((TOK, 384), BF16),
            pltpu.VMEM((2, 16, C), BF16),
            pltpu.VMEM((8, 16, C), BF16),
            pltpu.VMEM((3, TOK + 32, C), BF16),
            pltpu.VMEM((PER, NY, PAY_ROWS, 128), BF16),
            pltpu.VMEM((PER, NX, NY, PAY_ROWS, 128), BF16),
            pltpu.VMEM((6, HD, TOK), BF16),
            pltpu.VMEM((NZ, PER, HD, TOK), BF16),
            pltpu.VMEM((NX * NY * TOK, TOK), F32),
            pltpu.VMEM((NX * NY * TOK, TOK), F32),
            pltpu.VMEM((PER, NZ, O_ROWS, TOK), BF16),
            pltpu.VMEM((PER, NZ, O_ROWS, TOK), BF16),
            pltpu.VMEM((PER, HD, TOK), F32),
            pltpu.VMEM((NY, 64, 384), BF16),
            pltpu.VMEM((NY, 64, 384), BF16),
            dma((9,)),
            dma((8,)), dma((8,)),
            dma((4, 2)), dma((4, 2)),
            dma((PER, NY)), dma((PER, NY)),
            dma((PER, 2, 2)), dma((PER, 2, 2)),
            dma((PER, 2)), dma((PER, 2)),
            dma((PER, NZ)), dma((PER, NZ)),
            dma((NY,)), dma((NY,)),
        ],
        compiler_params=pltpu.CompilerParams(
            collective_id=0, has_side_effects=True, vmem_limit_bytes=63 * 2**20
        ),
    )(
        control.reshape(TOK, C),
        conv_weight.reshape(9, C, C),
        conv_bias,
        zero_weight,
        strengths,
        regions.reshape(-1),
        control_kv,
        base_kv.reshape(TOK, 2 * WIDE),
        queries.reshape(2 * TOK, WIDE),
    )
    return features.reshape(1, 16, 16, C), attended.reshape(1, 4, 16, WIDE)


def solution(mesh):
    in_specs = (
        P("img", "lat", "lon", None),
        P(),
        P(),
        P(),
        P(),
        P("img", None, "lon"),
        P(),
        P("img", "lat", "lon", None),
        P("img", None, "lon", None),
    )
    out_specs = (P("img", "lat", "lon", None), P("img", "lat", "lon", None))
    return jax.shard_map(body, mesh=mesh, in_specs=in_specs, out_specs=out_specs, check_vma=False)
```

```python
import jax
import jax.numpy as jnp
from jax import lax
from jax.experimental import pallas as pl
from jax.experimental.pallas import tpu as pltpu
from jax.sharding import PartitionSpec as P

F32, BF16 = jnp.float32, jnp.bfloat16
MESH = pl.DeviceIdType.MESH
NX, NY, NZ = 4, 4, 8
LON, LAT = 16, 8
TOK = 256
C = 320
HD = 64
HEADS = 20
PER = HEADS // NY
WIDE = HEADS * HD
PAIRS = NX * NY // 2
PAY_ROWS = TOK
O_ROWS = HD + 16
FIRST_TILES = (0, 2, 5, 7)
OTHER_TILES = (1, 3, 4, 6, 8, 9)


def dot(a, b):
    return jnp.dot(a, b, preferred_element_type=F32)


def kernel(
    ctl_h, cw_h, bias_h, zw_h, strg_h, reg_h, wkv_h, base_h, qin_h,
    feat, att,
    ctl, cw, bias, zw, strg, reg, wkv, base, qin,
    hs, hr, xs, pay, kv, qt, qb, s0, s1, osend, orecv, ct, fo, fr,
    in_s, h_s, h_r, q_s, q_r, y_s, y_r, x_s, x_r, w_s, w_r, o_s, o_r, f_s, f_r,
):
    lon, lat = lax.axis_index("lon"), lax.axis_index("lat")
    xh, z = lon // NZ, lon % NZ
    xl, y = lat // NY, lat % NY
    x = xh * 2 + xl
    right, left = (x + 1) % NX, (x + 3) % NX

    def at(px, py, pz):
        return {"lon": (px // 2) * NZ + pz, "lat": (px % 2) * NY + py}

    def remote(src, dst, send, recv, where):
        return pltpu.make_async_remote_copy(
            src_ref=src, dst_ref=dst, send_sem=send, recv_sem=recv, device_id=where, device_id_type=MESH
        )

    west, east = (lon + LON - 1) % LON, (lon + 1) % LON
    north, south = (lat + LAT - 1) % LAT, (lat + 1) % LAT
    around = (
        (west, north), (west, lat), (west, south),
        (east, north), (east, lat), (east, south),
        (lon, north), (lon, south),
    )

    def halo(k):
        src = hs.at[0] if k < 3 else hs.at[1] if k < 6 else ctl.at[pl.ds(0 if k == 6 else TOK - 16, 16)]
        return remote(src, hr.at[k], h_s.at[k], h_r.at[k], {"lon": around[k][0], "lat": around[k][1]})

    def q_part(step, k):
        tile = (z + NZ - step) % NZ if k == 0 else (z + step) % NZ
        if step < 3:
            return qb.at[tile]
        return qb.at[tile, pl.ds(0, 2)] if k == 0 else qb.at[tile, pl.ds(2, 3)]

    def q_send(step, k):
        ref = q_part(step, k)
        to = (z + 1) % NZ if k == 0 else (z + NZ - 1) % NZ
        return remote(ref, ref, q_s.at[step, k], q_r.at[step, k], at(x, y, to))

    def q_recv(step, k):
        tile = (z + NZ - step - 1) % NZ if k == 0 else (z + step + 1) % NZ
        ref = qb.at[tile] if step < 3 else qb.at[tile, pl.ds(0, 2)] if k == 0 else qb.at[tile, pl.ds(2, 3)]
        src = (z + NZ - 1) % NZ if k == 0 else (z + 1) % NZ
        return remote(ref, ref, q_s.at[step, k], q_r.at[step, k], at(x, y, src))

    def q_step(step):
        for k in range(2):
            if step > 0:
                q_recv(step - 1, k).wait_recv()
            q_send(step, k).start()

    def y_send(j, k):
        to = (y + k) % NY
        return remote(pay.at[j, to], kv.at[j, x, y], y_s.at[j, k], y_r.at[j, k], at(x, to, z))

    def y_recv(j, k):
        src = (y + NY - k) % NY
        return remote(kv.at[j, x, src], kv.at[j, x, src], y_s.at[j, k], y_r.at[j, k], at(x, src, z))

    def x_send(j, k, part):
        to = right if k == 0 else left
        ref = kv.at[j, x, pl.ds(2 * (k ^ part), 2)]
        return remote(ref, ref, x_s.at[j, k, part], x_r.at[j, k, part], at(to, y, z))

    def x_recv(j, k, part):
        src = left if k == 0 else right
        ref = kv.at[j, src, pl.ds(2 * (k ^ part), 2)]
        return remote(ref, ref, x_s.at[j, k, part], x_r.at[j, k, part], at(src, y, z))

    def w_send(j, k):
        slab, to = (left, right) if k == 0 else (right, left)
        ref = kv.at[j, slab, pl.ds(2 * k, 2)]
        return remote(ref, ref, w_s.at[j, k], w_r.at[j, k], at(to, y, z))

    def w_recv(j, k):
        ref = kv.at[j, (x + 2) % NX, pl.ds(2 * k, 2)]
        return remote(ref, ref, w_s.at[j, k], w_r.at[j, k], at(left if k == 0 else right, y, z))

    def o_send(j, k):
        return remote(osend.at[j, k], orecv.at[j, k], o_s.at[j, k], o_r.at[j, k], at(x, y, (z + k) % NZ))

    def f_send(k):
        to = (y + k) % NY
        return remote(fo.at[to], fr.at[y], f_s.at[k], f_r.at[k], at(x, to, z))

    def f_recv(k):
        src = (y + NY - k) % NY
        return remote(fr.at[src], fr.at[src], f_s.at[k], f_r.at[k], at(x, src, z))

    first_tile = (y * PER) // 2
    rows_q = pl.ds(pl.multiple_of(xl * TOK, TOK), TOK)
    lanes_q = pl.ds(pl.multiple_of(first_tile * 128, 128), 384)
    pairs_in = (
        (ctl_h, ctl), (qin_h.at[rows_q, lanes_q], qin), (cw_h, cw), (bias_h, bias), (zw_h, zw),
        (strg_h, strg), (reg_h, reg), (base_h, base), (wkv_h, wkv),
    )
    fetch = [pltpu.make_async_copy(a, b, in_s.at[n]) for n, (a, b) in enumerate(pairs_in)]
    for copy in fetch:
        copy.start()

    barrier = pltpu.get_barrier_semaphore()
    partners = [at(right, y, z), at(left, y, z)]
    partners += [at(x, (y + k) % NY, z) for k in range(1, NY)]
    partners += [at(x, y, (z + k) % NZ) for k in range(1, NZ)]
    partners += [{"lon": a, "lat": b} for a, b in around]
    for who in partners:
        pl.semaphore_signal(barrier, inc=1, device_id=who, device_id_type=MESH)

    fetch[0].wait()
    row16 = lax.broadcasted_iota(jnp.int32, (16, TOK), 0)
    col16 = lax.broadcasted_iota(jnp.int32, (16, TOK), 1)
    for side, off in ((0, 0), (1, 15)):
        pick = jnp.where(col16 == row16 * 16 + off, 1.0, 0.0).astype(BF16)
        hs[side] = dot(pick, ctl[...]).astype(BF16)

    fetch[1].wait()
    for t in range(3):
        turned = (qin[:, t * 128 : (t + 1) * 128].astype(F32).T * (HD**-0.5)).astype(BF16)
        qt[2 * t] = turned[:HD]
        qt[2 * t + 1] = turned[HD:]
    for j in range(PER):
        qb[z, j] = qt[(y * PER) % 2 + j]

    pl.semaphore_wait(barrier, len(partners))
    for k in range(8):
        halo(k).start()
    q_step(0)

    for k in range(8):
        halo(k).wait_recv()
    top = hr[7].astype(F32) * jnp.where(lat > 0, 1.0, 0.0)
    bottom = hr[6].astype(F32) * jnp.where(lat < LAT - 1, 1.0, 0.0)
    middle = jnp.concatenate([top, ctl[...].astype(F32), bottom], axis=0)
    tall = TOK + 32
    row = lax.broadcasted_iota(jnp.int32, (tall, 48), 0)
    pos = lax.broadcasted_iota(jnp.int32, (tall, 48), 1)
    first = jnp.where(lat > 0, 15, 16)
    last = jnp.where(lat < LAT - 1, 32, 31)
    wanted = (pos == row // 16 + 15) & (pos >= first) & (pos <= last)
    rows = lax.broadcasted_iota(jnp.int32, (tall, C), 0) % 16
    for tap, slots, edge, turn in ((0, (5, 4, 3), 0, 1), (2, (2, 1, 0), 15, tall - 1)):
        columns = jnp.concatenate([hr[s] for s in slots], axis=0)
        spread = dot(jnp.where(wanted & (row % 16 == edge), 1.0, 0.0).astype(BF16), columns)
        xs[tap] = jnp.where(rows == edge, spread, pltpu.roll(middle, turn, 0)).astype(BF16)
    xs[1] = middle.astype(BF16)
    for n in (2, 3, 4, 5, 6):
        fetch[n].wait()
    total = jnp.zeros((TOK, C), F32)
    for dr in range(3):
        for dc in range(3):
            total += dot(xs[dc, 16 * dr : 16 * dr + TOK], cw[3 * dr + dc])
    total += bias[...].reshape(1, C)
    active = (total / (1.0 + jnp.exp(-total))).astype(BF16)
    branch = dot(active, zw[...])
    strength = strg[reg[lat]]
    features = (ctl[...].astype(F32) + strength * branch).astype(BF16)
    feat[...] = features
    q_step(1)

    low = lax.broadcasted_iota(jnp.int32, (128, 128), 1) < HD

    def project(p):
        def part(col):
            out = base[:, col : col + 128].astype(F32) + dot(feat[...], wkv[:, col : col + 128])
            return out.astype(BF16).astype(F32)

        keys, turned = part(p * 128), part(WIDE + p * 128).T
        a, b = keys[:128], keys[128:]
        packed = (jnp.where(low, a, pltpu.roll(b, HD, 1)), jnp.where(low, pltpu.roll(a, HD, 1), b))
        for half in range(2):
            g, j = divmod(2 * p + half, PER)
            pay[j, g, 0:128] = packed[half].astype(BF16)
            pay[j, g, 128:192] = turned[half * HD : (half + 1) * HD, :128].astype(BF16)
            pay[j, g, 192:256] = turned[half * HD : (half + 1) * HD, 128:].astype(BF16)

    def y_out(j):
        for k in (2, 1, 3):
            y_send(j, k).start()
        kv[j, x, y] = pay[j, y]

    fetch[7].wait()
    fetch[8].wait()
    for p in FIRST_TILES:
        project(p)
    y_out(0)
    for p in OTHER_TILES:
        project(p)

    def spread_start(j):
        for k in range(1, NY):
            y_recv(j, k).wait_recv()
        for part in range(2):
            for k in range(2):
                x_send(j, k, part).start()

    def spread_more(j):
        for k in range(2):
            x_recv(j, k, 0).wait_recv()
            w_send(j, k).start()

    def spread_end(j):
        for k in range(2):
            x_recv(j, k, 1).wait_recv()
            w_recv(j, k).wait_recv()

    nothing = jnp.zeros((HD, TOK), BF16)
    ones = jnp.ones((16, TOK), BF16)

    def weights_of(j, k):
        q = qb[(z + k) % NZ, j]
        return jnp.concatenate(
            [jnp.concatenate([q, nothing], axis=0), jnp.concatenate([nothing, q], axis=0)], axis=1
        )

    def score(j, w, p, scores, peak):
        keys = kv[j, p // 2, 2 * (p % 2) : 2 * (p % 2) + 2, 0:128].reshape(TOK, 128)
        s = dot(keys, w)
        for half in range(2):
            part = s[:, half * TOK : (half + 1) * TOK]
            scores[(2 * p + half) * TOK : (2 * p + half + 1) * TOK] = part
            peak = jnp.maximum(peak, part.reshape(TOK // 8, 8, TOK).max(0))
        return peak

    def gather(j, p, scores, peak, acc):
        for half in range(2):
            s = scores[(2 * p + half) * TOK : (2 * p + half + 1) * TOK]
            weights = jnp.exp(s - peak).astype(BF16)
            begin = 128 + half * HD
            v = jnp.concatenate(
                [kv[j, p // 2, 2 * (p % 2) + u, begin : begin + HD] for u in range(2)], axis=1
            )
            acc += dot(jnp.concatenate([v, ones], axis=0), weights)
        return acc

    low_peak = jnp.full((8, TOK), -jnp.inf, F32)

    def packed_result(acc, peak):
        sums = acc[HD : HD + 1]
        log_sum = peak + jnp.log(sums)
        hi = log_sum.astype(BF16).astype(F32)
        mid = (log_sum - hi).astype(BF16).astype(F32)
        lo = log_sum - hi - mid
        r = lax.broadcasted_iota(jnp.int32, (16, TOK), 0)
        stats = jnp.where(r == 0, hi, jnp.where(r == 1, mid, jnp.where(r == 2, lo, 0.0)))
        return jnp.concatenate([acc[:HD] * (1.0 / sums), stats], axis=0).astype(BF16)

    def both(j, nj, nk, ready, coming, peak):
        w = weights_of(nj, nk)
        next_peak, acc = low_peak, jnp.zeros((O_ROWS, TOK), F32)
        for p in range(PAIRS):
            next_peak = score(nj, w, p, coming, next_peak)
            acc = gather(j, p, ready, peak, acc)
        return packed_result(acc, peak), next_peak.max(0, keepdims=True)

    def join(j):
        parts, logs = [], []
        for k in range(NZ):
            if k > 0:
                o_send(j, k).wait_recv()
            logs.append(orecv[j, k, HD : HD + 16].astype(F32)[0:3].sum(0, keepdims=True))
        top_log = logs[0]
        for other in logs[1:]:
            top_log = jnp.maximum(top_log, other)
        out, whole = jnp.zeros((HD, TOK), F32), jnp.zeros((1, TOK), F32)
        for k in range(NZ):
            share = jnp.exp(logs[k] - top_log)
            whole += share
            out += orecv[j, k, 0:HD].astype(F32) * share
        ct[j] = out * (1.0 / whole)

    spread_start(0)
    lax.fori_loop(1, PER, lambda j, _: (y_out(j), 0)[1], 0)
    q_step(2)
    spread_more(0)
    spread_start(1)
    q_step(3)
    spread_end(0)
    for k in range(2):
        q_recv(3, k).wait_recv()
    w = weights_of(0, 4)
    peak = low_peak
    for p in range(PAIRS):
        peak = score(0, w, p, s0, peak)
    peak = peak.max(0, keepdims=True)

    def step(n, peak):
        j, i = n // 4, n % 4
        more = j < PER - 1

        @pl.when((i == 1) & more)
        def _():
            spread_more(j + 1)

        @pl.when((i == 1) & (j < PER - 2))
        def _():
            spread_start(j + 2)

        @pl.when((i == 2) & (j > 0))
        def _():
            join(j - 1)

        result, peak = both(j, j, 3 - i, s0, s1, peak)
        osend[j, 4 + i] = result
        o_send(j, 4 + i).start()

        @pl.when((i == 3) & more)
        def _():
            spread_end(j + 1)

        nj = jnp.where((i == 3) & more, j + 1, j)
        nk = jnp.where(i == 3, 4, 5 + i)
        result, peak = both(j, nj, nk, s1, s0, peak)

        @pl.when(i < 3)
        def _():
            osend[j, 3 - i] = result
            o_send(j, 3 - i).start()

        @pl.when(i == 3)
        def _():
            orecv[j, 0] = result

        return peak

    lax.fori_loop(0, 4 * PER, step, peak)
    join(PER - 1)

    for t in range(3):
        if t < 2:
            turned = jnp.concatenate([ct[2 * t], ct[2 * t + 1]], axis=0).T
        else:
            turned = jnp.concatenate([ct[4], jnp.zeros((HD, TOK), F32)], axis=0).T
        for g in range(NY):
            fo[g, :, t * 128 : (t + 1) * 128] = turned[g * 64 : (g + 1) * 64].astype(BF16)
    for k in (2, 1, 3):
        f_send(k).start()
    fr[y] = fo[y]
    for k in range(1, NY):
        f_recv(k).wait_recv()
    att[...] = jnp.concatenate([fr[g][:, :C].astype(F32) for g in range(NY)], axis=1).astype(BF16)

    for k in range(8):
        halo(k).wait_send()

    for step in range(4):
        for k in range(2):
            q_send(step, k).wait_send()

    def drain(j, _):
        for k in range(1, NZ):
            o_send(j, k).wait_send()
        for k in range(1, NY):
            y_send(j, k).wait_send()
        for k in range(2):
            x_send(j, k, 0).wait_send()
            x_send(j, k, 1).wait_send()
            w_send(j, k).wait_send()
        return 0

    lax.fori_loop(0, PER, drain, 0)
    for k in range(1, NY):
        f_send(k).wait_send()


def body(control, conv_weight, conv_bias, zero_weight, strengths, regions, control_kv, base_kv, queries):
    vmem = pl.BlockSpec(memory_space=pltpu.VMEM)
    hbm = pl.BlockSpec(memory_space=pltpu.HBM)
    dma = pltpu.SemaphoreType.DMA
    features, attended = pl.pallas_call(
        kernel,
        out_shape=[
            jax.ShapeDtypeStruct((TOK, C), BF16),
            jax.ShapeDtypeStruct((64, WIDE), BF16),
        ],
        in_specs=[hbm] * 9,
        out_specs=[vmem, vmem],
        scratch_shapes=[
            pltpu.VMEM((TOK, C), BF16),
            pltpu.VMEM((9, C, C), BF16),
            pltpu.VMEM((C,), F32),
            pltpu.VMEM((C, C), BF16),
            pltpu.SMEM((8,), F32),
            pltpu.SMEM((8,), jnp.int32),
            pltpu.VMEM((C, 2 * WIDE), BF16),
            pltpu.VMEM((TOK, 2 * WIDE), BF16),
            pltpu.VMEM((TOK, 384), BF16),
            pltpu.VMEM((2, 16, C), BF16),
            pltpu.VMEM((8, 16, C), BF16),
            pltpu.VMEM((3, TOK + 32, C), BF16),
            pltpu.VMEM((PER, NY, PAY_ROWS, 128), BF16),
            pltpu.VMEM((PER, NX, NY, PAY_ROWS, 128), BF16),
            pltpu.VMEM((6, HD, TOK), BF16),
            pltpu.VMEM((NZ, PER, HD, TOK), BF16),
            pltpu.VMEM((NX * NY * TOK, TOK), F32),
            pltpu.VMEM((NX * NY * TOK, TOK), F32),
            pltpu.VMEM((PER, NZ, O_ROWS, TOK), BF16),
            pltpu.VMEM((PER, NZ, O_ROWS, TOK), BF16),
            pltpu.VMEM((PER, HD, TOK), F32),
            pltpu.VMEM((NY, 64, 384), BF16),
            pltpu.VMEM((NY, 64, 384), BF16),
            dma((9,)),
            dma((8,)), dma((8,)),
            dma((4, 2)), dma((4, 2)),
            dma((PER, NY)), dma((PER, NY)),
            dma((PER, 2, 2)), dma((PER, 2, 2)),
            dma((PER, 2)), dma((PER, 2)),
            dma((PER, NZ)), dma((PER, NZ)),
            dma((NY,)), dma((NY,)),
        ],
        compiler_params=pltpu.CompilerParams(
            collective_id=0, has_side_effects=True, vmem_limit_bytes=54 * 2**20
        ),
    )(
        control.reshape(TOK, C),
        conv_weight.reshape(9, C, C),
        conv_bias,
        zero_weight,
        strengths,
        regions.reshape(-1),
        control_kv,
        base_kv.reshape(TOK, 2 * WIDE),
        queries.reshape(2 * TOK, WIDE),
    )
    return features.reshape(1, 16, 16, C), attended.reshape(1, 4, 16, WIDE)


def solution(mesh):
    in_specs = (
        P("img", "lat", "lon", None),
        P(),
        P(),
        P(),
        P(),
        P("img", None, "lon"),
        P(),
        P("img", "lat", "lon", None),
        P("img", None, "lon", None),
    )
    out_specs = (P("img", "lat", "lon", None), P("img", "lat", "lon", None))
    return jax.shard_map(body, mesh=mesh, in_specs=in_specs, out_specs=out_specs, check_vma=False)
```
